256 devices in a mesh: expert: 16 (over y, x), mp: 16 (over z, core).
Axes of the slice: x: 4, y: 4, z: 8, core: 2. Of those that a mesh axis runs over, the one named last changes fastest.
Arguments:
- tokens: bfloat16 [8192, 4096], P('expert', 'mp'), may hold values from -6 to 6
- gate_prob: float32 [8192], P('expert'), may hold values from 0.2 to 1
- expert_index: int32 [8192], P('expert'), may hold values from 0 to 15, as said below
- slot_index: int32 [8192], P('expert'), may hold values from 0 to 40, as said below
- weight_in: bfloat16 [16, 4096, 5120], P('expert', None, 'mp'), may hold values from -0.125 to 0.125
- weight_out: bfloat16 [16, 5120, 4096], P('expert', 'mp'), may hold values from -0.125 to 0.125
- grad_output: bfloat16 [8192, 4096], P('expert', 'mp'), may hold values from -1.5 to 1.5
Outputs:
- layer_out: bfloat16 [8192, 4096], P('expert', 'mp')
- grad_tokens: bfloat16 [8192, 4096], P('expert', 'mp')
- grad_gate: float32 [8192], P('expert')
- grad_weight_in: bfloat16 [16, 4096, 5120], P('expert', None, 'mp')
- grad_weight_out: bfloat16 [16, 5120, 4096], P('expert', 'mp')
The draws below stay inside these ranges and needn't reach their ends.
Inputs may be any that keep to these rules, and one draw needn't show every extreme that they name: `expert_index`: in every block of 512 tokens some expert is chosen by more than 40 tokens. `slot_index`: among the tokens of one block that choose one expert, slots 0, 1, 2, ... are given once each in an order of priority; every token beyond the first 40 of them gets 40 and is dropped.
All inputs are finite; a program needn't handle non-finite values.
Results may differ from the reference program's by a relative error of at most 0.023.
Values may be sent and summed in bfloat16 or wider, within the bound.
No kernel may reach another device: no remote copies, remote signals or barrier semaphores. Data moves between devices by JAX's collectives and lax.ppermute only.
A program may use at most 128 MiB of HBM per device.

```python
import math
import jax
import jax.numpy as jnp
from jax import lax

D = 4096
FF = 5120
TOK_DEV = 512
EXPERTS = 16
TOKENS = 8192
CAP = 40
N_MP = 16


def route_table(key):
    blocks = TOKENS // TOK_DEV
    labels = jax.random.permutation(jax.random.fold_in(key, 101), EXPERTS).astype(jnp.int32)

    def one_block(block_key):
        sub_keys = jax.random.split(block_key, 4)
        first = jax.random.randint(sub_keys[0], (TOK_DEV,), 0, EXPERTS)
        second = jax.random.randint(sub_keys[1], (TOK_DEV,), 0, EXPERTS)
        order = jnp.arange(TOK_DEV, dtype=jnp.int32)
        raw_expert = jnp.where(order < CAP + 1, 0, jnp.minimum(first, second)).astype(jnp.int32)
        raw_expert = jax.random.permutation(sub_keys[2], raw_expert)
        priority = jax.random.permutation(sub_keys[3], TOK_DEV)
        same_expert = raw_expert[:, None] == raw_expert[None, :]
        before = priority[None, :] < priority[:, None]
        rank_in = jnp.sum(same_expert & before, axis=1).astype(jnp.int32)
        return (labels[raw_expert].astype(jnp.int32), jnp.minimum(rank_in, CAP).astype(jnp.int32))
    block_keys = jax.random.split(jax.random.fold_in(key, 202), blocks)
    experts_drawn, slots_drawn = jax.vmap(one_block)(block_keys)
    return (experts_drawn.reshape(-1), slots_drawn.reshape(-1))


def draw_expert_index(key, part):
    drawn_pair = route_table(key)
    return drawn_pair[0]


def draw_slot_index(key, part):
    drawn_pair = route_table(key)
    return drawn_pair[1]


def strengthened(array, stream_key, source, target, parts, factor):
    def block_of(dim):
        return (jnp.arange(array.shape[dim]) // (array.shape[dim] // parts)).reshape((-1,) + (1,) * (array.ndim - 1 - dim))

    near = jax.random.permutation(stream_key, parts)[block_of(target)]
    other_side = (block_of(target) + parts // 2) % parts
    return jnp.where((block_of(source) == near) | (block_of(source) == other_side), factor * array, array)


def block_levels(own_key, dims, shards, least, high):
    loudness, own = 1.0, jax.random.fold_in(own_key, 6)
    for dim, parts in shards:
        draws = jnp.exp(jax.random.uniform(jax.random.fold_in(own, dim), (parts,), jnp.float32, least / len(shards), high / len(shards)))
        loudness = loudness * jnp.repeat(draws, dims[dim] // parts).reshape([-1 if axis == dim else 1 for axis in range(len(dims))])
    return loudness


def scatter_about(own_key, extent, scale, reach, shards=(), kind=jnp.bfloat16):
    array = jax.random.normal(own_key, extent, jnp.float32) * scale
    if len(shards) > 0:
        array = block_levels(own_key, extent, shards, -0.22, 0.18) * array
    return jnp.clip(array, min=-reach, max=reach).astype(kind)


def bell_draw_with(rng, shape, width, bound, cuts, heavy, held_as=jnp.bfloat16):
    values = width * jax.random.normal(rng, shape, jnp.float32)
    if cuts:
        values = values * block_levels(rng, shape, cuts, -0.22, 0.18)
    return jnp.clip(strengthened(values, jax.random.fold_in(rng, 3), *heavy), -bound, bound).astype(held_as)


def setup_inputs(seed: int = 0) -> dict:
    key_list = jax.random.split(jax.random.key(seed), 8)
    return {
        "tokens": scatter_about(key_list[0], (TOKENS, D), 1.0, 6.0, ((0, 16), (1, 16))),
        "gate_prob": jnp.clip(jnp.exp(math.log(1.0) - 1.609438 * jax.random.uniform(key_list[1], (TOKENS,), jnp.float32) ** block_levels(key_list[1], (TOKENS,), ((0, 16),), -0.2, 0.2)), 0.2, 1.0),
        "expert_index": draw_expert_index(jax.random.fold_in(key_list[7], 71), 0),
        "slot_index": draw_slot_index(jax.random.fold_in(key_list[7], 71), 0),
        "weight_in": bell_draw_with(key_list[4], (EXPERTS, D, FF), D ** -0.5, 0.125, ((0, 16), (2, 16)), (2, 1, 16, 2.0)),
        "weight_out": bell_draw_with(key_list[5], (EXPERTS, FF, D), FF ** -0.5, 0.125, ((0, 16), (1, 16)), (1, 2, 16, 2.0)),
        "grad_output": scatter_about(key_list[6], (TOKENS, D), 0.25, 1.5, ((0, 16), (1, 16))),
    }


tanh_scale = 0.7978845608028654
cubic_coef = 0.044715


def gelu_tanh(value):
    inner = tanh_scale * (value + cubic_coef * value * value * value)
    return 0.5 * value * (1.0 + jnp.tanh(inner))


def gelu_slope(value):
    inner = tanh_scale * (value + cubic_coef * value * value * value)
    squash = jnp.tanh(inner)
    return 0.5 * (1.0 + squash) + 0.5 * value * (1.0 - squash * squash) * tanh_scale * (1.0 + 3.0 * cubic_coef * value * value)


def sliced_product(left, right):
    piece_width = FF // N_MP

    def add_piece(index, total):
        start = (index * piece_width).astype(jnp.int32)
        left_part = lax.dynamic_slice_in_dim(left, start, piece_width, 1)
        right_part = lax.dynamic_slice_in_dim(right, start, piece_width, 0)
        term = jnp.dot(left_part, right_part, preferred_element_type=jnp.float32).astype(jnp.bfloat16)
        return total + term.astype(jnp.float32)

    empty = jnp.zeros((left.shape[0], right.shape[1]), jnp.float32)
    return lax.fori_loop(jnp.int32(0), jnp.int32(N_MP), add_piece, empty)


def reference(tokens, gate_prob, expert_index, slot_index, weight_in, weight_out, grad_output):
    buffer_rows = (TOKENS // TOK_DEV) * CAP
    block_of = jnp.arange(TOKENS, dtype=jnp.int32) // TOK_DEV
    is_kept = slot_index < CAP
    position = (block_of * CAP + jnp.minimum(slot_index, CAP - 1)).astype(jnp.int32)
    scaled_grad = (gate_prob[:, None] * grad_output.astype(jnp.float32)).astype(jnp.bfloat16)
    grad_wide = grad_output.astype(jnp.float32)

    def per_expert(carry, expert_id):
        out_acc, grad_acc, gate_acc = carry
        is_mine = (expert_index == expert_id) & is_kept
        destination = jnp.where(is_mine, position, buffer_rows).astype(jnp.int32)
        empty = jnp.zeros((buffer_rows, D), jnp.bfloat16)
        expert_rows = empty.at[destination].set(tokens, mode="drop")
        grad_rows = empty.at[destination].set(scaled_grad, mode="drop")
        inner_weight = weight_in[expert_id]
        outer_weight = weight_out[expert_id]
        pre_act = jnp.dot(expert_rows, inner_weight, preferred_element_type=jnp.float32)
        activation = gelu_tanh(pre_act).astype(jnp.bfloat16)
        expert_out = sliced_product(activation, outer_weight).astype(jnp.bfloat16)
        grad_act = jnp.dot(grad_rows, outer_weight.T, preferred_element_type=jnp.float32)
        grad_pre = (grad_act * gelu_slope(pre_act)).astype(jnp.bfloat16)
        grad_outer = jnp.dot(activation.T, grad_rows, preferred_element_type=jnp.float32).astype(jnp.bfloat16)
        grad_inner = jnp.dot(expert_rows.T, grad_pre, preferred_element_type=jnp.float32).astype(jnp.bfloat16)
        grad_back = sliced_product(grad_pre, inner_weight.T).astype(jnp.bfloat16)
        picked = expert_out[position].astype(jnp.float32)
        out_acc = jnp.where(is_mine[:, None], gate_prob[:, None] * picked, out_acc)
        gate_acc = jnp.where(is_mine, jnp.sum(grad_wide * picked, axis=1), gate_acc)
        back_picked = grad_back[position].astype(jnp.float32)
        grad_acc = jnp.where(is_mine[:, None], gate_prob[:, None] * back_picked, grad_acc)
        return (out_acc, grad_acc, gate_acc), (grad_inner, grad_outer)

    start = (jnp.zeros((TOKENS, D), jnp.float32), jnp.zeros((TOKENS, D), jnp.float32), jnp.zeros((TOKENS,), jnp.float32))
    finals, stacked = lax.scan(per_expert, start, jnp.arange(EXPERTS, dtype=jnp.int32))
    out_acc, grad_acc, gate_acc = finals
    grad_weight_in, grad_weight_out = stacked
    return (out_acc.astype(jnp.bfloat16), grad_acc.astype(jnp.bfloat16), gate_acc, grad_weight_in, grad_weight_out)
```

```python
import functools

import jax
import jax.numpy as jnp
from jax import lax
from jax.experimental import pallas as pl
from jax.experimental.pallas import tpu as pltpu
from jax.sharding import PartitionSpec as P

tanh_scale = 0.7978845608028654
cubic_coef = 0.044715
CAP = 40
NZ = 8
VMEM_LIMIT = 56 * 1024 * 1024
F32 = jnp.float32
BF16 = jnp.bfloat16
WHOLE = pl.BlockSpec(memory_space=pltpu.VMEM)
SCALARS = pl.BlockSpec(memory_space=pltpu.SMEM)


def dot(left, right, left_dim=1, right_dim=0):
    return lax.dot_general(
        left, right, (((left_dim,), (right_dim,)), ((), ())), preferred_element_type=F32
    )


def call(kernel, out_shape, operands, flops, in_specs=None):
    moved = sum(a.size * a.dtype.itemsize for a in operands) + sum(
        a.size * a.dtype.itemsize for a in out_shape
    )
    return pl.pallas_call(
        kernel,
        out_shape=out_shape,
        in_specs=in_specs or [WHOLE] * len(operands),
        out_specs=[WHOLE] * len(out_shape),
        compiler_params=pltpu.CompilerParams(vmem_limit_bytes=VMEM_LIMIT),
        cost_estimate=pl.CostEstimate(flops=flops, bytes_accessed=moved, transcendentals=0),
    )(*operands)


def shape(dims, dtype=BF16):
    return jax.ShapeDtypeStruct(dims, dtype)


def dispatch_kernel(dest_ref, gate_ref, tokens_ref, grad_ref, rows_ref, grows_ref):
    rows, count = rows_ref.shape[0], tokens_ref.shape[0]
    pick = (lax.broadcasted_iota(jnp.int32, (rows, count), 0) == dest_ref[...]).astype(BF16)
    rows_ref[...] = dot(pick, tokens_ref[...]).astype(BF16)
    scaled = (gate_ref[...] * grad_ref[...].astype(F32)).astype(BF16)
    grows_ref[...] = dot(pick, scaled).astype(BF16)


def chunk(refs, offset):
    if offset < 4:
        return refs[offset][...]
    if offset > 4:
        return refs[offset - 1][...]
    return jnp.concatenate([refs[7][...], refs[8][...]], 0)


def block_of(order_ref, offset, side, width):
    return pl.ds(pl.multiple_of(order_ref[side * NZ + offset] * width, width), width)


def forward_kernel(order_ref, *refs):
    sides, (inner_ref, outer_ref), (own_ref, other_ref, act_ref, slope_ref, acc_ref) = (
        (refs[:9], refs[9:18]),
        refs[18:20],
        refs[20:],
    )
    width = own_ref.shape[2]
    for side in range(2):
        for offset in range(NZ):
            term = dot(
                chunk(sides[side], offset), inner_ref[block_of(order_ref, offset, side, width), :]
            )
            if side == 0 and offset == 0:
                acc_ref[...] = term
            else:
                acc_ref[...] += term
    value = acc_ref[...]
    inner = tanh_scale * (value + cubic_coef * value * value * value)
    squash = jnp.tanh(inner)
    act_ref[...] = (0.5 * value * (1.0 + squash)).astype(BF16)
    slope_ref[...] = 0.5 * (1.0 + squash) + 0.5 * value * (1.0 - squash * squash) * tanh_scale * (
        1.0 + 3.0 * cubic_coef * value * value
    )
    for offset in (4, 3, 5, 2, 6, 1, 7, 0):
        for side, out_ref in ((1, other_ref), (0, own_ref)):
            out_ref[offset] = dot(
                act_ref[...], outer_ref[:, block_of(order_ref, offset, side, width)]
            ).astype(BF16)


def backward_kernel(order_ref, *refs):
    sides, (inner_ref, outer_ref, act_ref, slope_ref), (own_ref, other_ref, pre_ref, acc_ref) = (
        (refs[:9], refs[9:18]),
        refs[18:22],
        refs[22:],
    )
    rows, width = act_ref.shape[0], own_ref.shape[2]
    for side in range(2):
        for offset in range(NZ):
            term = dot(
                chunk(sides[side], offset),
                outer_ref[:, block_of(order_ref, offset, side, width)],
                1,
                1,
            )
            if side == 0 and offset == 0:
                acc_ref[...] = term
            else:
                acc_ref[...] += term
    grad_act = acc_ref[...]
    pre_ref[...] = (grad_act * slope_ref[...]).astype(BF16)
    gate = jnp.sum(grad_act * act_ref[...].astype(F32), axis=1, keepdims=True)
    groups = rows // CAP
    row = lax.broadcasted_iota(jnp.int32, (rows, width), 0)
    lane = lax.broadcasted_iota(jnp.int32, (rows, width), 1)
    spread = jnp.where(row % CAP == lane, gate, 0.0).astype(BF16)
    member = (
        lax.broadcasted_iota(jnp.int32, (groups, rows), 1) // CAP
        == lax.broadcasted_iota(jnp.int32, (groups, rows), 0)
    ).astype(BF16)
    gate_rows = dot(member, spread).astype(BF16)
    for offset in (4, 3, 5, 2, 6, 1, 7, 0):
        for side, out_ref in ((1, other_ref), (0, own_ref)):
            out_ref[offset, :rows] = dot(
                pre_ref[...], inner_ref[block_of(order_ref, offset, side, width), :], 1, 1
            ).astype(BF16)
            out_ref[offset, rows:] = gate_rows


def outer_grad_kernel(order_ref, *refs):
    sides, act_ref, out_ref = (refs[:9], refs[9:18]), refs[18], refs[19]
    width = refs[0].shape[1]
    for side in range(2):
        for offset in range(NZ):
            out_ref[:, block_of(order_ref, offset, side, width)] = dot(
                act_ref[...], chunk(sides[side], offset), 0, 0
            ).astype(BF16)


def inner_grad_kernel(order_ref, *refs):
    sides, pre_ref, out_ref = (refs[:9], refs[9:18]), refs[18], refs[19]
    width = refs[0].shape[1]
    for side in range(2):
        for offset in range(NZ):
            out_ref[block_of(order_ref, offset, side, width), :] = dot(
                chunk(sides[side], offset), pre_ref[...], 0, 0
            ).astype(BF16)


def layer_kernel(pos_ref, scale_ref, back_ref, out_ref):
    count, rows = pos_ref.shape[0], back_ref.shape[0]
    pick = (lax.broadcasted_iota(jnp.int32, (count, rows), 1) == pos_ref[...]).astype(BF16)
    out_ref[...] = (scale_ref[...] * dot(pick, back_ref[...])).astype(BF16)


def permute(array, pairs):
    return lax.ppermute(array, "mp", pairs)


def ring_pairs():
    count = 2 * NZ
    up = [(i, (i + 2) % count) for i in range(count)]
    down = [(i, (i - 2) % count) for i in range(count)]
    swap = [(i, i ^ 1) for i in range(count)]
    return up, down, swap


def gather_ring(shard):
    up, down, swap = ring_pairs()
    half = shard.shape[0] // 2
    own = [None] * 9
    own[0] = going_up = going_down = shard
    for step in (1, 2, 3):
        going_up, going_down = permute(going_up, up), permute(going_down, down)
        own[step], own[7 - step] = going_down, going_up
    own[7] = permute(going_up[:half], up)
    own[8] = permute(going_down[half:], down)
    return own + [permute(part, swap) for part in own]


def reduce_ring(own, other):
    up, down, swap = ring_pairs()
    rows = own.shape[1]
    half = rows // 2
    near = permute(other, swap)

    def local(offset):
        return own[offset % NZ].astype(F32) + near[offset % NZ].astype(F32)

    going_up = permute(local(4)[:half].astype(BF16), up)
    going_down = permute(local(4)[half:].astype(BF16), down)
    mine = local(3)
    up_sum = jnp.concatenate([mine[:half] + going_up.astype(F32), mine[half:]], 0)
    mine = local(-3)
    down_sum = jnp.concatenate([mine[:half], mine[half:] + going_down.astype(F32)], 0)
    for step in (2, 1, 0):
        going_up = permute(up_sum.astype(BF16), up)
        going_down = permute(down_sum.astype(BF16), down)
        up_sum = local(step) + going_up.astype(F32)
        down_sum = local(-step) + going_down.astype(F32)
    return (local(0) + going_up.astype(F32) + going_down.astype(F32)).astype(BF16)


def exchange(array):
    return lax.all_to_all(array, "expert", split_axis=0, concat_axis=0, tiled=True)


def body(tokens, gate_prob, expert_index, slot_index, weight_in, weight_out, grad_output):
    count, width = tokens.shape
    groups = lax.axis_size("expert")
    rows = groups * CAP
    inner, outer = weight_in[0], weight_out[0]
    hidden = inner.shape[1]
    me = lax.axis_index("mp")
    z, core = me // 2, me % 2
    spots = (z + jnp.arange(NZ)) % NZ
    order = jnp.concatenate([2 * spots + core, 2 * spots + 1 - core]).astype(jnp.int32)
    kept = slot_index < CAP
    place = jnp.where(kept, expert_index * CAP + slot_index, rows).astype(jnp.int32)
    gate_column = gate_prob[:, None]
    send_rows, send_grads = call(
        dispatch_kernel,
        [shape((rows, width))] * 2,
        (place[None, :], gate_column, tokens, grad_output),
        4 * rows * count * width,
    )
    got_rows = exchange(send_rows.reshape(groups, CAP, width)).reshape(rows, width)
    got_grads = exchange(send_grads.reshape(groups, CAP, width)).reshape(rows, width)
    x_parts = gather_ring(got_rows)
    g_parts = gather_ring(got_grads)
    product = 2 * rows * hidden * inner.shape[0]
    own, other, act, slope = pl.pallas_call(
        forward_kernel,
        out_shape=[
            shape((NZ, rows, width)),
            shape((NZ, rows, width)),
            shape((rows, hidden)),
            shape((rows, hidden), F32),
        ],
        in_specs=[SCALARS] + [WHOLE] * 20,
        out_specs=[WHOLE] * 4,
        scratch_shapes=[pltpu.VMEM((rows, hidden), F32)],
        compiler_params=pltpu.CompilerParams(vmem_limit_bytes=VMEM_LIMIT),
        cost_estimate=pl.CostEstimate(
            flops=2 * product, bytes_accessed=16 << 20, transcendentals=0
        ),
    )(order, *x_parts, inner, outer)
    out_share = reduce_ring(own, other)
    tall = rows + groups
    own, other, pre = pl.pallas_call(
        backward_kernel,
        out_shape=[
            shape((NZ, tall, width)),
            shape((NZ, tall, width)),
            shape((rows, hidden)),
        ],
        in_specs=[SCALARS] + [WHOLE] * 22,
        out_specs=[WHOLE] * 3,
        scratch_shapes=[pltpu.VMEM((rows, hidden), F32)],
        compiler_params=pltpu.CompilerParams(vmem_limit_bytes=VMEM_LIMIT),
        cost_estimate=pl.CostEstimate(
            flops=2 * product, bytes_accessed=16 << 20, transcendentals=0
        ),
    )(order, *g_parts, inner, outer, act, slope)
    back_share = reduce_ring(own, other)
    (grad_outer,) = call(
        outer_grad_kernel,
        [shape(outer.shape)],
        (order, *g_parts, act),
        product,
        [SCALARS] + [WHOLE] * 19,
    )
    (grad_inner,) = call(
        inner_grad_kernel,
        [shape(inner.shape)],
        (order, *x_parts, pre),
        product,
        [SCALARS] + [WHOLE] * 19,
    )
    out_back = exchange(out_share.reshape(groups, CAP, width)).reshape(rows, width)
    extra = jnp.pad(back_share[rows:].reshape(groups, 1, width), ((0, 0), (0, 7), (0, 0)))
    back = exchange(
        jnp.concatenate([back_share[:rows].reshape(groups, CAP, width), extra], 1)
    )
    back_rows = back[:, :CAP].reshape(rows, width)
    gate_table = back[:, CAP, :CAP].reshape(rows)
    scale = jnp.where(kept, gate_prob, 0.0)[:, None]
    place_column = place[:, None]
    (layer_out,) = call(
        layer_kernel,
        [shape((count, width))],
        (place_column, scale, out_back),
        2 * rows * count * width,
    )
    (grad_tokens,) = call(
        layer_kernel,
        [shape((count, width))],
        (place_column, scale, back_rows),
        2 * rows * count * width,
    )
    gate_sum = gate_table[jnp.minimum(place, rows - 1)].astype(F32)
    grad_gate = jnp.where(kept, gate_sum / gate_prob, 0.0)
    return (layer_out, grad_tokens, grad_gate, grad_inner[None], grad_outer[None])


def solution(mesh):
    in_specs = (
        P("expert", "mp"),
        P("expert"),
        P("expert"),
        P("expert"),
        P("expert", None, "mp"),
        P("expert", "mp", None),
        P("expert", "mp"),
    )
    out_specs = (
        P("expert", "mp"),
        P("expert", "mp"),
        P("expert"),
        P("expert", None, "mp"),
        P("expert", "mp", None),
    )
    return jax.shard_map(body, mesh=mesh, in_specs=in_specs, out_specs=out_specs, check_vma=False)
```

```python
import functools

import functools

import jax
import jax.numpy as jnp
from jax import lax
from jax.experimental import pallas as pl
from jax.experimental.pallas import tpu as pltpu
from jax.sharding import PartitionSpec as P

tanh_scale = 0.7978845608028654
cubic_coef = 0.044715
CAP = 40
NZ = 8
VMEM_LIMIT = 6 * 1024 * 1024
F32 = jnp.float32
BF16 = jnp.bfloat16
WHOLE = pl.BlockSpec(memory_space=pltpu.VMEM)
SCALARS = pl.BlockSpec(memory_space=pltpu.SMEM)


def dot(left, right, left_dim=1, right_dim=0):
    return lax.dot_general(
        left, right, (((left_dim,), (right_dim,)), ((), ())), preferred_element_type=F32
    )


ANY = pl.BlockSpec(memory_space=pl.ANY)
FAR = pl.BlockSpec(memory_space=pltpu.HBM)
FIRST = (3, 4, 5)
REST = (0, 1, 2, 6, 7)


def shape(dims, dtype=BF16):
    return jax.ShapeDtypeStruct(dims, dtype)


def call(
    kernel, out_shape, operands, in_specs, out_specs, scratch, flops, vmem=VMEM_LIMIT
):
    return pl.pallas_call(
        kernel,
        out_shape=out_shape,
        in_specs=in_specs,
        out_specs=out_specs,
        scratch_shapes=scratch,
        compiler_params=pltpu.CompilerParams(vmem_limit_bytes=vmem),
        cost_estimate=pl.CostEstimate(flops=1, bytes_accessed=1, transcendentals=0),
    )(*operands)


def column(row):
    lanes = 128
    return jnp.broadcast_to(row, (lanes, row.shape[1])).T[:, :1]


def place_of(expert, slot, rows):
    return jnp.where(slot < CAP, expert * CAP + slot, rows)


def dispatch_kernel(expert_ref, slot_ref, gate_ref, tokens_ref, grad_ref, send_ref, *scratch):
    expert, slot, gate, tokens, grad, send, sems = scratch
    width, rows, count = tokens.shape[1], send.shape[0], tokens.shape[0]
    loads = [
        pltpu.make_async_copy(source, target, sems.at[i])
        for i, (source, target) in enumerate(
            (
                (expert_ref, expert),
                (slot_ref, slot),
                (gate_ref, gate),
                (tokens_ref, tokens),
                (grad_ref, grad),
            )
        )
    ]
    for load in loads:
        load.start()
    for load in loads:
        load.wait()
    place = place_of(expert[...], slot[...], rows)
    pick = lax.broadcasted_iota(jnp.int32, (rows, count), 0) == place
    scale = jnp.sum(jnp.where(pick, gate[...], 0.0), axis=1, keepdims=True)
    pick = pick.astype(BF16)
    send[:, :width] = dot(pick, tokens[...]).astype(BF16)
    send[:, width:] = (scale * dot(pick, grad[...])).astype(BF16)
    store = pltpu.make_async_copy(send, send_ref, sems.at[len(loads)])
    store.start()
    store.wait()


def relative_kernel(order_ref, inner_ref, outer_ref, inner_out, outer_out, sems):
    width = inner_out.shape[2]
    copies = []
    for i in range(2 * NZ):
        spot = pl.ds(pl.multiple_of(order_ref[i] * width, width), width)
        for j, (ref, out) in enumerate(((inner_ref, inner_out), (outer_ref, outer_out))):
            copies.append(pltpu.make_async_copy(ref.at[:, spot], out.at[i], sems.at[j, i]))
    for copy in copies:
        copy.start()
    for copy in copies:
        copy.wait()


STEPS = (
    ((0, 0, 0, 0), (1, 0, 0, 1), (2, 0, 1, 0), (3, 0, 7, 0), (4, 0, 1, 1), (4, 1, 7, 1)),
    ((0, 0, 2, 0), (1, 0, 6, 0), (2, 0, 2, 1), (2, 1, 6, 1)),
    ((0, 0, 3, 0), (1, 0, 5, 0), (2, 0, 3, 1), (2, 1, 5, 1)),
    ((0, 0, 4, 0), (1, 0, 4, 1)),
)
COUNTS = (5, 3, 3, 2)


def product_of(step, parts, weight_ref, part_rows):
    rows, total = parts[0].shape[0], None
    for i, block, offset, side in STEPS[step]:
        part = parts[i][pl.ds(block * rows + part_rows.start, part_rows.size)]
        term = dot(part, weight_ref[side * NZ + offset], 1, 1)
        total = term if total is None else total + term
    return total


def by_halves(ref, compute):
    half = ref.shape[0] // 2

    def one(i, carry):
        spot = pl.ds(pl.multiple_of(i * half, half), half)
        ref[spot] = compute(spot)
        return carry

    lax.fori_loop(0, 2, one, 0)


def first_kernel(weight_ref, *refs):
    by_halves(refs[-1], lambda spot: product_of(0, refs[:-1], weight_ref, spot))


def more_kernel(step, weight_ref, acc_ref, *refs):
    by_halves(
        refs[-1], lambda spot: acc_ref[spot] + product_of(step, refs[:-1], weight_ref, spot)
    )


def expand(offsets, left_ref, weight_ref, out_refs, extra=None):
    rows = left_ref.shape[0]

    def one(i, carry):
        offset = i + 3 if offsets == FIRST else i + jnp.where(i > 2, 3, 0)
        for side in (1, 0):
            out_refs[side][i, :rows] = dot(left_ref[...], weight_ref[side * NZ + offset]).astype(
                BF16
            )
            if extra is not None:
                out_refs[side][i, rows:] = extra
        return carry

    lax.fori_loop(0, len(offsets), one, 0)


def forward_kernel(inner_ref, outer_ref, acc_ref, *refs):
    own_ref, other_ref, act_ref, slope_ref = refs[2:]
    every = pl.ds(0, acc_ref.shape[0])
    value = acc_ref[...] + product_of(3, refs[:2], inner_ref, every)
    inner = tanh_scale * (value + cubic_coef * value * value * value)
    squash = jnp.tanh(inner)
    act_ref[...] = (0.5 * value * (1.0 + squash)).astype(BF16)
    slope_ref[...] = 0.5 * (1.0 + squash) + 0.5 * value * (1.0 - squash * squash) * tanh_scale * (
        1.0 + 3.0 * cubic_coef * value * value
    )
    expand(FIRST, act_ref, outer_ref, (own_ref, other_ref))


def gate_rows_of(grad_act, act, width):
    rows = act.shape[0]
    gate = jnp.sum(grad_act * act.astype(F32), axis=1, keepdims=True)
    groups = rows // CAP
    row = lax.broadcasted_iota(jnp.int32, (rows, width), 0)
    lane = lax.broadcasted_iota(jnp.int32, (rows, width), 1)
    spread = jnp.where(row % CAP == lane, gate, 0.0).astype(BF16)
    start = CAP * lax.broadcasted_iota(jnp.int32, (groups, rows), 0)
    spot = lax.broadcasted_iota(jnp.int32, (groups, rows), 1)
    member = ((spot >= start) & (spot < start + CAP)).astype(BF16)
    return dot(member, spread).astype(BF16)


def backward_kernel(inner_ref, outer_ref, acc_ref, act_ref, slope_ref, *refs):
    own_ref, other_ref, pre_ref, gate_ref = refs[2:]
    width = own_ref.shape[2]
    every = pl.ds(0, acc_ref.shape[0])
    grad_act = acc_ref[...] + product_of(3, refs[:2], outer_ref, every)
    pre_ref[...] = (grad_act * slope_ref[...]).astype(BF16)
    gate_ref[...] = gate_rows_of(grad_act, act_ref[...], width)
    expand(FIRST, pre_ref, inner_ref, (own_ref, other_ref), gate_ref[...])


def rest_kernel(left_ref, weight_ref, *refs):
    extra = refs[0][...] if len(refs) == 3 else None
    expand(REST, left_ref, weight_ref, refs[-2:], extra)


def weight_grad_kernel(order_ref, left_ref, *refs):
    total = sum(COUNTS)
    parts, (out_ref, stage_ref, sems) = refs[:total], refs[total:]
    left = left_ref[...].T
    rows, width = left.shape[1], stage_ref.shape[2]
    copies = []
    for step, blocks in enumerate(STEPS):
        first = sum(COUNTS[:step])
        for i, block, offset, side in blocks:
            part = parts[first + i][block * rows : (block + 1) * rows]
            stage_ref[side * NZ + offset] = dot(left, part).astype(BF16)
        for _, _, offset, side in blocks:
            spot = side * NZ + offset
            where = pl.ds(pl.multiple_of(order_ref[spot] * width, width), width)
            copy = pltpu.make_async_copy(stage_ref.at[spot], out_ref.at[:, where], sems.at[spot])
            copy.start()
            copies.append(copy)
    for copy in copies:
        copy.wait()


def layer_kernel(expert_ref, slot_ref, gate_ref, back_ref, out_ref):
    count, rows = out_ref.shape[0], back_ref.shape[0]
    place = column(place_of(expert_ref[...], slot_ref[...], rows))
    pick = (lax.broadcasted_iota(jnp.int32, (count, rows), 1) == place).astype(BF16)
    out_ref[...] = (column(gate_ref[...]) * dot(pick, back_ref[...])).astype(BF16)


def final_kernel(expert_ref, slot_ref, gate_ref, back_ref, out_ref, grad_gate_ref):
    count, groups, width = out_ref.shape[0], back_ref.shape[0], back_ref.shape[2]
    rows = groups * CAP
    expert, slot = column(expert_ref[...]), column(slot_ref[...])
    place = place_of(expert, slot, rows)
    pick = (lax.broadcasted_iota(jnp.int32, (count, rows), 1) == place).astype(BF16)
    back = back_ref[:, :CAP, :].reshape(rows, width)
    out_ref[...] = (column(gate_ref[...]) * dot(pick, back)).astype(BF16)
    group = (lax.broadcasted_iota(jnp.int32, (count, groups), 1) == expert).astype(BF16)
    table = dot(group, back_ref[:, CAP, :])
    lane = lax.broadcasted_iota(jnp.int32, (count, width), 1)
    sums = jnp.sum(jnp.where((lane == slot) & (slot < CAP), table, 0.0), axis=1, keepdims=True)
    sums = jnp.broadcast_to(sums, (count, 128)).T[:1]
    grad_gate_ref[...] = sums / gate_ref[...]


def permute(array, pairs):
    return lax.ppermute(array, "mp", pairs)


def ring_pairs():
    count = 2 * NZ
    up = [(i, (i + 2) % count) for i in range(count)]
    down = [(i, (i - 2) % count) for i in range(count)]
    swap = [(i, i ^ 1) for i in range(count)]
    return up, down, swap


def after(value, *others):
    return lax.optimization_barrier((value, *others))[0]


def gather_ring(shard, take, leads=(None,) * 4):
    up, down, swap = ring_pairs()
    half = shard.shape[0] // 2
    swapped = permute(shard, swap)
    going_up = going_down = shard
    marks, taken, total = [], [], None
    for step in range(3):
        if leads[step] is not None:
            going_up, going_down = after(going_up, leads[step]), after(going_down, leads[step])
        going_up, going_down = permute(going_up, up), permute(going_down, down)
        going_up, going_down = lax.optimization_barrier((going_up, going_down))
        marks.append(going_up)
        parts = [going_down, going_up]
        parts.append(permute(jnp.concatenate(parts, 0), swap))
        if step == 0:
            parts = [shard, swapped] + parts
        before, total = total, take(step, total, parts)
        taken += parts
        if before is not None:
            going_up, going_down = after(going_up, before), after(going_down, before)
    if leads[3] is not None:
        going_up, going_down = after(going_up, leads[3]), after(going_down, leads[3])
    far_up, far_down = permute(going_up[:half], up), permute(going_down[half:], down)
    marks.append(far_up)
    far = jnp.concatenate([far_up, far_down], 0)
    return total, taken, [far, permute(far, swap)], marks


def reduce_ring(own_first, other_first, own_rest, other_rest, waits):
    up, down, swap = ring_pairs()
    rows = own_first.shape[1]
    half = rows // 2
    near_first, near_rest = permute(other_first, swap), permute(other_rest, swap)

    def local(offset, part=slice(None)):
        if offset in FIRST:
            i = FIRST.index(offset)
            return own_first[i, part].astype(F32) + near_first[i, part].astype(F32)
        i = REST.index(offset)
        return own_rest[i, part].astype(F32) + near_rest[i, part].astype(F32)

    top, bottom = slice(0, half), slice(half, rows)
    up_sum, down_sum = local(4, top), local(4, bottom)
    marks = []
    for step in (3, 2, 1, 0):
        up_sum, down_sum = up_sum.astype(BF16), down_sum.astype(BF16)
        if step in waits:
            up_sum, down_sum = lax.optimization_barrier((up_sum, down_sum, waits[step](marks)))[:2]
        going_up, going_down = permute(up_sum, up), permute(down_sum, down)
        going_up, going_down = lax.optimization_barrier((going_up, going_down))
        marks.append(going_up)
        if step == 3:
            up_sum = jnp.concatenate([local(3, top) + going_up.astype(F32), local(3, bottom)], 0)
            down_sum = jnp.concatenate(
                [local(5, top), local(5, bottom) + going_down.astype(F32)], 0
            )
        elif step > 0:
            up_sum = local(step) + going_up.astype(F32)
            down_sum = local(NZ - step) + going_down.astype(F32)
    share = (local(0) + going_up.astype(F32) + going_down.astype(F32)).astype(BF16)
    return share, marks


def exchange(array):
    return lax.all_to_all(array, "expert", split_axis=0, concat_axis=0, tiled=True)


def body(tokens, gate_prob, expert_index, slot_index, weight_in, weight_out, grad_output):
    count, width = tokens.shape
    groups = lax.axis_size("expert")
    rows = groups * CAP
    inner, outer = weight_in[0].T, weight_out[0]
    hidden = inner.shape[0]
    me = lax.axis_index("mp")
    z, core = me // 2, me % 2
    spots = (z + jnp.arange(NZ)) % NZ
    order = jnp.concatenate([2 * spots + core, 2 * spots + 1 - core]).astype(jnp.int32)
    expert_row, slot_row, gate_row = expert_index[None], slot_index[None], gate_prob[None]
    picked = 2 * rows * count * width
    blocks = shape((2 * NZ, hidden, width))
    (send,) = call(
        dispatch_kernel,
        [shape((rows, 2 * width))],
        (expert_row, slot_row, gate_row, tokens, grad_output),
        [FAR] * 5,
        [ANY],
        [
            pltpu.VMEM((1, count), jnp.int32),
            pltpu.VMEM((1, count), jnp.int32),
            pltpu.VMEM((1, count), F32),
            pltpu.VMEM((count, width), BF16),
            pltpu.VMEM((count, width), BF16),
            pltpu.VMEM((rows, 2 * width), BF16),
            pltpu.SemaphoreType.DMA((6,)),
        ],
        2 * picked,
        57 << 20,
    )
    inner_rel, outer_rel = call(
        relative_kernel,
        [blocks] * 2,
        (order, inner, outer),
        [SCALARS, ANY, ANY],
        [WHOLE] * 2,
        [pltpu.SemaphoreType.DMA((2, 2 * NZ))],
        0,
    )
    got = exchange(send.reshape(groups, CAP, 2 * width)).reshape(rows, 2 * width)
    got_rows, got_grads = got[:, :width], got[:, width:]
    product = 2 * rows * hidden * inner.shape[1]
    tall = rows + groups
    total_shape = shape((rows, hidden), F32)
    def taker(weight):
        def take(step, total, parts):
            flops = product * len(parts) // 16
            if step == 0:
                return call(
                    first_kernel,
                    [total_shape],
                    (weight, *parts),
                    [WHOLE] * (1 + len(parts)),
                    [WHOLE],
                    [],
                    flops,
                )[0]
            return call(
                functools.partial(more_kernel, step),
                [total_shape],
                (weight, total, *parts),
                [WHOLE] * (2 + len(parts)),
                [WHOLE],
                [],
                flops,
            )[0]

        return take

    def rest(left, weight, height, *extra):
        return call(
            rest_kernel,
            [shape((len(REST), height, width))] * 2,
            (left, weight, *extra),
            [WHOLE] * (2 + len(extra)),
            [WHOLE] * 2,
            [],
            product * len(REST) // NZ,
        )

    def weight_grad(parts, left):
        return call(
            weight_grad_kernel,
            [shape(outer.shape)],
            (order, left, *parts),
            [SCALARS] + [WHOLE] * (1 + len(parts)),
            [ANY],
            [
                pltpu.VMEM((2 * NZ, hidden, width), BF16),
                pltpu.SemaphoreType.DMA((2 * NZ,)),
            ],
            product,
        )[0]

    x_total, x_parts, x_far, marks = gather_ring(got_rows, taker(inner_rel))
    g_total, g_parts, g_far, _ = gather_ring(got_grads, taker(outer_rel), (marks[0], None, None, None))
    own, other, act, slope = call(
        forward_kernel,
        [
            shape((len(FIRST), rows, width)),
            shape((len(FIRST), rows, width)),
            shape((rows, hidden)),
            total_shape,
        ],
        (inner_rel, outer_rel, x_total, *x_far),
        [WHOLE] * 5,
        [WHOLE] * 4,
        [],
        product // 2,
    )
    rest_pieces = rest(act, outer_rel, rows)
    grads = {}

    def outer_grad(marks):
        grads["outer"] = weight_grad(g_parts + g_far, after(act, marks[0]))
        return grads["outer"]

    def inner_grad(marks):
        grads["inner"] = weight_grad(x_parts + x_far, after(pre, marks[1]))
        return grads["inner"]

    out_first = own, other
    own, other, pre, gate_rows = call(
        backward_kernel,
        [
            shape((len(FIRST), tall, width)),
            shape((len(FIRST), tall, width)),
            shape((rows, hidden)),
            shape((groups, width)),
        ],
        (inner_rel, outer_rel, g_total, act, slope, *g_far),
        [WHOLE] * 7,
        [WHOLE] * 4,
        [],
        product // 2,
    )
    back_pieces = rest(pre, inner_rel, tall, gate_rows)
    out_share, _ = reduce_ring(*out_first, *rest_pieces, {1: outer_grad, 0: inner_grad})
    back_share, _ = reduce_ring(own, other, *back_pieces, {})
    grad_inner, grad_outer = grads["inner"], grads["outer"]
    grad_inner = grad_inner.T
    out_back = exchange(out_share.reshape(groups, CAP, width)).reshape(rows, width)
    (layer_out,) = call(
        layer_kernel,
        [shape((count, width))],
        (expert_row, slot_row, gate_row, out_back),
        [WHOLE] * 4,
        [WHOLE],
        [],
        picked,
    )
    extra = jnp.pad(back_share[rows:].reshape(groups, 1, width), ((0, 0), (0, 7), (0, 0)))
    back = exchange(
        jnp.concatenate([back_share[:rows].reshape(groups, CAP, width), extra], 1)
    )
    grad_tokens, grad_gate = call(
        final_kernel,
        [shape((count, width)), shape((1, count), F32)],
        (expert_row, slot_row, gate_row, back),
        [WHOLE] * 4,
        [WHOLE] * 2,
        [],
        picked,
    )
    return (layer_out, grad_tokens, grad_gate[0], grad_inner[None], grad_outer[None])


def solution(mesh):
    in_specs = (
        P("expert", "mp"),
        P("expert"),
        P("expert"),
        P("expert"),
        P("expert", None, "mp"),
        P("expert", "mp", None),
        P("expert", "mp"),
    )
    out_specs = (
        P("expert", "mp"),
        P("expert", "mp"),
        P("expert"),
        P("expert", None, "mp"),
        P("expert", "mp", None),
    )
    return jax.shard_map(body, mesh=mesh, in_specs=in_specs, out_specs=out_specs, check_vma=False)
```

```python
import functools

import functools

import jax
import jax.numpy as jnp
from jax import lax
from jax.experimental import pallas as pl
from jax.experimental.pallas import tpu as pltpu
from jax.sharding import PartitionSpec as P

tanh_scale = 0.7978845608028654
cubic_coef = 0.044715
CAP = 40
NZ = 8
VMEM_LIMIT = 6 * 1024 * 1024
F32 = jnp.float32
BF16 = jnp.bfloat16
WHOLE = pl.BlockSpec(memory_space=pltpu.VMEM)
SCALARS = pl.BlockSpec(memory_space=pltpu.SMEM)


def dot(left, right, left_dim=1, right_dim=0):
    return lax.dot_general(
        left, right, (((left_dim,), (right_dim,)), ((), ())), preferred_element_type=F32
    )


ANY = pl.BlockSpec(memory_space=pl.ANY)
FAR = pl.BlockSpec(memory_space=pltpu.HBM)
FIRST = (3, 4, 5)
REST = (0, 1, 2, 6, 7)


def shape(dims, dtype=BF16):
    return jax.ShapeDtypeStruct(dims, dtype)


def call(
    kernel, out_shape, operands, in_specs, out_specs, scratch, flops, vmem=VMEM_LIMIT
):
    return pl.pallas_call(
        kernel,
        out_shape=out_shape,
        in_specs=in_specs,
        out_specs=out_specs,
        scratch_shapes=scratch,
        compiler_params=pltpu.CompilerParams(vmem_limit_bytes=vmem),
        cost_estimate=pl.CostEstimate(flops=1, bytes_accessed=1, transcendentals=0),
    )(*operands)


def column(row):
    lanes = 128
    return jnp.broadcast_to(row, (lanes, row.shape[1])).T[:, :1]


def place_of(expert, slot, rows):
    return jnp.where(slot < CAP, expert * CAP + slot, rows)


def dispatch_kernel(expert_ref, slot_ref, gate_ref, tokens_ref, grad_ref, send_ref, *scratch):
    expert, slot, gate, tokens, grad, send, sems = scratch
    width, rows, count = tokens.shape[1], send.shape[0], tokens.shape[0]
    loads = [
        pltpu.make_async_copy(source, target, sems.at[i])
        for i, (source, target) in enumerate(
            (
                (expert_ref, expert),
                (slot_ref, slot),
                (gate_ref, gate),
                (tokens_ref, tokens),
                (grad_ref, grad),
            )
        )
    ]
    for load in loads:
        load.start()
    for load in loads:
        load.wait()
    place = place_of(expert[...], slot[...], rows)
    pick = lax.broadcasted_iota(jnp.int32, (rows, count), 0) == place
    scale = jnp.sum(jnp.where(pick, gate[...], 0.0), axis=1, keepdims=True)
    pick = pick.astype(BF16)
    send[:, :width] = dot(pick, tokens[...]).astype(BF16)
    send[:, width:] = (scale * dot(pick, grad[...])).astype(BF16)
    store = pltpu.make_async_copy(send, send_ref, sems.at[len(loads)])
    store.start()
    store.wait()


def relative_kernel(order_ref, inner_ref, outer_ref, inner_out, outer_out, sems):
    width = inner_out.shape[2]
    copies = []
    for i in range(2 * NZ):
        spot = pl.ds(pl.multiple_of(order_ref[i] * width, width), width)
        for j, (ref, out) in enumerate(((inner_ref, inner_out), (outer_ref, outer_out))):
            copies.append(pltpu.make_async_copy(ref.at[:, spot], out.at[i], sems.at[j, i]))
    for copy in copies:
        copy.start()
    for copy in copies:
        copy.wait()


STEPS = (
    ((0, 0, 0, 0), (1, 0, 0, 1), (2, 0, 1, 0), (3, 0, 7, 0), (4, 0, 1, 1), (4, 1, 7, 1)),
    ((0, 0, 2, 0), (1, 0, 6, 0), (2, 0, 2, 1), (2, 1, 6, 1)),
    ((0, 0, 3, 0), (1, 0, 5, 0), (2, 0, 3, 1), (2, 1, 5, 1)),
    ((0, 0, 4, 0), (1, 0, 4, 1)),
)
COUNTS = (5, 3, 3, 2)


def product_of(step, parts, weight_ref, part_rows):
    rows, total = parts[0].shape[0], None
    for i, block, offset, side in STEPS[step]:
        part = parts[i][pl.ds(block * rows + part_rows.start, part_rows.size)]
        term = dot(part, weight_ref[side * NZ + offset], 1, 1)
        total = term if total is None else total + term
    return total


def by_halves(ref, compute):
    half = ref.shape[0] // 2

    def one(i, carry):
        spot = pl.ds(pl.multiple_of(i * half, half), half)
        ref[spot] = compute(spot)
        return carry

    lax.fori_loop(0, 2, one, 0)


def first_kernel(weight_ref, *refs):
    by_halves(refs[-1], lambda spot: product_of(0, refs[:-1], weight_ref, spot))


def more_kernel(step, weight_ref, acc_ref, *refs):
    by_halves(
        refs[-1], lambda spot: acc_ref[spot] + product_of(step, refs[:-1], weight_ref, spot)
    )


def expand(offsets, left_ref, weight_ref, out_refs, extra=None):
    rows = left_ref.shape[0]

    def one(i, carry):
        offset = i + 3 if offsets == FIRST else i + jnp.where(i > 2, 3, 0)
        for side in (1, 0):
            out_refs[side][i, :rows] = dot(left_ref[...], weight_ref[side * NZ + offset]).astype(
                BF16
            )
            if extra is not None:
                out_refs[side][i, rows:] = extra
        return carry

    lax.fori_loop(0, len(offsets), one, 0)


def forward_kernel(inner_ref, outer_ref, acc_ref, *refs):
    own_ref, other_ref, act_ref, slope_ref = refs[2:]
    every = pl.ds(0, acc_ref.shape[0])
    value = acc_ref[...] + product_of(3, refs[:2], inner_ref, every)
    inner = tanh_scale * (value + cubic_coef * value * value * value)
    squash = jnp.tanh(inner)
    act_ref[...] = (0.5 * value * (1.0 + squash)).astype(BF16)
    slope_ref[...] = 0.5 * (1.0 + squash) + 0.5 * value * (1.0 - squash * squash) * tanh_scale * (
        1.0 + 3.0 * cubic_coef * value * value
    )
    expand(FIRST, act_ref, outer_ref, (own_ref, other_ref))


def gate_rows_of(grad_act, act, width):
    rows = act.shape[0]
    gate = jnp.sum(grad_act * act.astype(F32), axis=1, keepdims=True)
    groups = rows // CAP
    row = lax.broadcasted_iota(jnp.int32, (rows, width), 0)
    lane = lax.broadcasted_iota(jnp.int32, (rows, width), 1)
    spread = jnp.where(row % CAP == lane, gate, 0.0).astype(BF16)
    start = CAP * lax.broadcasted_iota(jnp.int32, (groups, rows), 0)
    spot = lax.broadcasted_iota(jnp.int32, (groups, rows), 1)
    member = ((spot >= start) & (spot < start + CAP)).astype(BF16)
    return dot(member, spread).astype(BF16)


def backward_kernel(inner_ref, outer_ref, acc_ref, act_ref, slope_ref, *refs):
    own_ref, other_ref, pre_ref, gate_ref = refs[2:]
    width = own_ref.shape[2]
    every = pl.ds(0, acc_ref.shape[0])
    grad_act = acc_ref[...] + product_of(3, refs[:2], outer_ref, every)
    pre_ref[...] = (grad_act * slope_ref[...]).astype(BF16)
    gate_ref[...] = gate_rows_of(grad_act, act_ref[...], width)
    expand(FIRST, pre_ref, inner_ref, (own_ref, other_ref), gate_ref[...])


def rest_kernel(left_ref, weight_ref, *refs):
    extra = refs[0][...] if len(refs) == 3 else None
    expand(REST, left_ref, weight_ref, refs[-2:], extra)


def weight_grad_kernel(order_ref, left_ref, *refs):
    total = sum(COUNTS)
    parts, (out_ref, stage_ref, sems) = refs[:total], refs[total:]
    left = left_ref[...].T
    rows, width = left.shape[1], stage_ref.shape[2]
    copies = []
    for step, blocks in enumerate(STEPS):
        first = sum(COUNTS[:step])
        for i, block, offset, side in blocks:
            part = parts[first + i][block * rows : (block + 1) * rows]
            stage_ref[side * NZ + offset] = dot(left, part).astype(BF16)
        for _, _, offset, side in blocks:
            spot = side * NZ + offset
            where = pl.ds(pl.multiple_of(order_ref[spot] * width, width), width)
            copy = pltpu.make_async_copy(stage_ref.at[spot], out_ref.at[:, where], sems.at[spot])
            copy.start()
            copies.append(copy)
    for copy in copies:
        copy.wait()


def layer_kernel(expert_ref, slot_ref, gate_ref, back_ref, out_ref):
    count, rows = out_ref.shape[0], back_ref.shape[0]
    place = column(place_of(expert_ref[...], slot_ref[...], rows))
    pick = (lax.broadcasted_iota(jnp.int32, (count, rows), 1) == place).astype(BF16)
    out_ref[...] = (column(gate_ref[...]) * dot(pick, back_ref[...])).astype(BF16)


def final_kernel(expert_ref, slot_ref, gate_ref, back_ref, out_ref, grad_gate_ref):
    count, groups, tall, width = out_ref.shape[0], *back_ref.shape
    rows = groups * tall
    expert, slot = column(expert_ref[...]), column(slot_ref[...])
    place = jnp.where(slot < CAP, expert * tall + slot, rows)
    spot = lax.broadcasted_iota(jnp.int32, (count, rows), 1)
    back = back_ref[...].reshape(rows, width)
    out_ref[...] = (column(gate_ref[...]) * dot((spot == place).astype(BF16), back)).astype(BF16)
    table = dot((spot == expert * tall + CAP).astype(BF16), back)
    lane = lax.broadcasted_iota(jnp.int32, (count, width), 1)
    sums = jnp.sum(jnp.where((lane == slot) & (slot < CAP), table, 0.0), axis=1, keepdims=True)
    sums = jnp.broadcast_to(sums, (count, 128)).T[:1]
    grad_gate_ref[...] = sums / gate_ref[...]


def permute(array, pairs):
    return lax.ppermute(array, "mp", pairs)


def ring_pairs():
    count = 2 * NZ
    up = [(i, (i + 2) % count) for i in range(count)]
    down = [(i, (i - 2) % count) for i in range(count)]
    swap = [(i, i ^ 1) for i in range(count)]
    return up, down, swap


def after(value, *others):
    return lax.optimization_barrier((value, *others))[0]


def gather_ring(shard, take, leads=(None,) * 4):
    up, down, swap = ring_pairs()
    half = shard.shape[0] // 2
    swapped = permute(shard, swap)
    going_up = going_down = shard
    marks, taken, total = [], [], None
    for step in range(3):
        if leads[step] is not None:
            going_up, going_down = after(going_up, leads[step]), after(going_down, leads[step])
        going_up, going_down = permute(going_up, up), permute(going_down, down)
        going_up, going_down = lax.optimization_barrier((going_up, going_down))
        marks.append(going_up)
        parts = [going_down, going_up]
        parts.append(permute(jnp.concatenate(parts, 0), swap))
        if step == 0:
            parts = [shard, swapped] + parts
        before, total = total, take(step, total, parts)
        taken += parts
        if before is not None:
            going_up, going_down = after(going_up, before), after(going_down, before)
    if leads[3] is not None:
        going_up, going_down = after(going_up, leads[3]), after(going_down, leads[3])
    far_up, far_down = permute(going_up[:half], up), permute(going_down[half:], down)
    marks.append(far_up)
    far = jnp.concatenate([far_up, far_down], 0)
    return total, taken, [far, permute(far, swap)], marks


def reduce_ring(own_first, other_first, own_rest, other_rest, waits):
    up, down, swap = ring_pairs()
    rows = own_first.shape[1]
    half = rows // 2
    near_first, near_rest = permute(other_first, swap), permute(other_rest, swap)

    def local(offset, part=slice(None)):
        if offset in FIRST:
            i = FIRST.index(offset)
            return own_first[i, part].astype(F32) + near_first[i, part].astype(F32)
        i = REST.index(offset)
        return own_rest[i, part].astype(F32) + near_rest[i, part].astype(F32)

    top, bottom = slice(0, half), slice(half, rows)
    up_sum, down_sum = local(4, top), local(4, bottom)
    marks = []
    for step in (3, 2, 1, 0):
        up_sum, down_sum = up_sum.astype(BF16), down_sum.astype(BF16)
        if step in waits:
            up_sum, down_sum = lax.optimization_barrier((up_sum, down_sum, waits[step](marks)))[:2]
        going_up, going_down = permute(up_sum, up), permute(down_sum, down)
        going_up, going_down = lax.optimization_barrier((going_up, going_down))
        marks.append(going_up)
        if step == 3:
            up_sum = jnp.concatenate([local(3, top) + going_up.astype(F32), local(3, bottom)], 0)
            down_sum = jnp.concatenate(
                [local(5, top), local(5, bottom) + going_down.astype(F32)], 0
            )
        elif step > 0:
            up_sum = local(step) + going_up.astype(F32)
            down_sum = local(NZ - step) + going_down.astype(F32)
    share = (local(0) + going_up.astype(F32) + going_down.astype(F32)).astype(BF16)
    return share, marks


def exchange(array):
    return lax.all_to_all(array, "expert", split_axis=0, concat_axis=0, tiled=True)


def body(tokens, gate_prob, expert_index, slot_index, weight_in, weight_out, grad_output):
    count, width = tokens.shape
    groups = lax.axis_size("expert")
    rows = groups * CAP
    inner, outer = weight_in[0].T, weight_out[0]
    hidden = inner.shape[0]
    me = lax.axis_index("mp")
    z, core = me // 2, me % 2
    spots = (z + jnp.arange(NZ)) % NZ
    order = jnp.concatenate([2 * spots + core, 2 * spots + 1 - core]).astype(jnp.int32)
    expert_row, slot_row, gate_row = expert_index[None], slot_index[None], gate_prob[None]
    picked = 2 * rows * count * width
    blocks = shape((2 * NZ, hidden, width))
    (send,) = call(
        dispatch_kernel,
        [shape((rows, 2 * width))],
        (expert_row, slot_row, gate_row, tokens, grad_output),
        [FAR] * 5,
        [ANY],
        [
            pltpu.VMEM((1, count), jnp.int32),
            pltpu.VMEM((1, count), jnp.int32),
            pltpu.VMEM((1, count), F32),
            pltpu.VMEM((count, width), BF16),
            pltpu.VMEM((count, width), BF16),
            pltpu.VMEM((rows, 2 * width), BF16),
            pltpu.SemaphoreType.DMA((6,)),
        ],
        2 * picked,
        57 << 20,
    )
    inner_rel, outer_rel = call(
        relative_kernel,
        [blocks] * 2,
        (order, inner, outer),
        [SCALARS, ANY, ANY],
        [WHOLE] * 2,
        [pltpu.SemaphoreType.DMA((2, 2 * NZ))],
        0,
    )
    got = exchange(send.reshape(groups, CAP, 2 * width)).reshape(rows, 2 * width)
    got_rows, got_grads = got[:, :width], got[:, width:]
    product = 2 * rows * hidden * inner.shape[1]
    tall = rows + groups
    total_shape = shape((rows, hidden), F32)
    def taker(weight):
        def take(step, total, parts):
            flops = product * len(parts) // 16
            if step == 0:
                return call(
                    first_kernel,
                    [total_shape],
                    (weight, *parts),
                    [WHOLE] * (1 + len(parts)),
                    [WHOLE],
                    [],
                    flops,
                )[0]
            return call(
                functools.partial(more_kernel, step),
                [total_shape],
                (weight, total, *parts),
                [WHOLE] * (2 + len(parts)),
                [WHOLE],
                [],
                flops,
            )[0]

        return take

    def rest(left, weight, height, *extra):
        return call(
            rest_kernel,
            [shape((len(REST), height, width))] * 2,
            (left, weight, *extra),
            [WHOLE] * (2 + len(extra)),
            [WHOLE] * 2,
            [],
            product * len(REST) // NZ,
        )

    def weight_grad(parts, left):
        return call(
            weight_grad_kernel,
            [shape(outer.shape)],
            (order, left, *parts),
            [SCALARS] + [WHOLE] * (1 + len(parts)),
            [ANY],
            [
                pltpu.VMEM((2 * NZ, hidden, width), BF16),
                pltpu.SemaphoreType.DMA((2 * NZ,)),
            ],
            product,
        )[0]

    x_total, x_parts, x_far, marks = gather_ring(got_rows, taker(inner_rel))
    g_total, g_parts, g_far, _ = gather_ring(got_grads, taker(outer_rel), (marks[0], None, None, None))
    own, other, act, slope = call(
        forward_kernel,
        [
            shape((len(FIRST), rows, width)),
            shape((len(FIRST), rows, width)),
            shape((rows, hidden)),
            total_shape,
        ],
        (inner_rel, outer_rel, x_total, *x_far),
        [WHOLE] * 5,
        [WHOLE] * 4,
        [],
        product // 2,
    )
    rest_pieces = rest(act, outer_rel, rows)
    grads = {}

    def outer_grad(marks):
        grads["outer"] = weight_grad(g_parts + g_far, after(act, marks[0]))
        return grads["outer"]

    def inner_grad(marks):
        grads["inner"] = weight_grad(x_parts + x_far, after(pre, marks[1]))
        return grads["inner"]

    out_first = own, other
    own, other, pre, gate_rows = call(
        backward_kernel,
        [
            shape((len(FIRST), tall, width)),
            shape((len(FIRST), tall, width)),
            shape((rows, hidden)),
            shape((groups, width)),
        ],
        (inner_rel, outer_rel, g_total, act, slope, *g_far),
        [WHOLE] * 7,
        [WHOLE] * 4,
        [],
        product // 2,
    )
    back_pieces = rest(pre, inner_rel, tall, gate_rows)
    out_share, _ = reduce_ring(*out_first, *rest_pieces, {1: outer_grad, 0: inner_grad})
    back_share, _ = reduce_ring(own, other, *back_pieces, {})
    grad_inner, grad_outer = grads["inner"], grads["outer"]
    grad_inner = grad_inner.T
    out_back = exchange(out_share.reshape(groups, CAP, width)).reshape(rows, width)
    (layer_out,) = call(
        layer_kernel,
        [shape((count, width))],
        (expert_row, slot_row, gate_row, out_back),
        [WHOLE] * 4,
        [WHOLE],
        [],
        picked,
    )
    extra = jnp.pad(back_share[rows:].reshape(groups, 1, width), ((0, 0), (0, 7), (0, 0)))
    back = exchange(
        jnp.concatenate([back_share[:rows].reshape(groups, CAP, width), extra], 1)
    )
    grad_tokens, grad_gate = call(
        final_kernel,
        [shape((count, width)), shape((1, count), F32)],
        (expert_row, slot_row, gate_row, back),
        [WHOLE] * 4,
        [WHOLE] * 2,
        [],
        picked,
    )
    return (layer_out, grad_tokens, grad_gate[0], grad_inner[None], grad_outer[None])


def solution(mesh):
    in_specs = (
        P("expert", "mp"),
        P("expert"),
        P("expert"),
        P("expert"),
        P("expert", None, "mp"),
        P("expert", "mp", None),
        P("expert", "mp"),
    )
    out_specs = (
        P("expert", "mp"),
        P("expert", "mp"),
        P("expert"),
        P("expert", None, "mp"),
        P("expert", "mp", None),
    )
    return jax.shard_map(body, mesh=mesh, in_specs=in_specs, out_specs=out_specs, check_vma=False)
```
